512 devices in a mesh: dom: 128 (over y, z, core), row: 4 (over x).
Axes of the slice: x: 4, y: 8, z: 8, core: 2. Of those that a mesh axis runs over, the one named last changes fastest.
Arguments:
- p_blocks: bfloat16 [1536, 12, 128, 128], P(('dom', 'row')), may hold values from -0.5 to 0.5
- p_cols: int32 [1536, 12], P(('dom', 'row')), may hold values from 0 to 1535, as said below
- sel_square: int32 [1536, 4, 12], P(('dom', 'row')), may hold values from -1 to 1, as said below
- sel_cube: int32 [1536, 4, 12], P(('dom', 'row')), may hold values from -1 to 3, as said below
Outputs:
- purified: bfloat16 [1536, 4, 128, 128], P(('dom', 'row'))
The draws below stay inside these ranges and needn't reach their ends.
Inputs may be any that keep to these rules, and one draw needn't show every extreme that they name: `p_cols`: the 12 entries of a row are distinct clusters held by devices at most 2 positions away from the row's own device in dom-then-row order, cyclically. `sel_square`: -1 marks a term left out; other values name one of the first 2 stored blocks of row p_cols[i, a]. `sel_cube`: -1 marks a term left out; other values name a block of square of row p_cols[i, a].
All inputs are finite; a program needn't handle non-finite values.
Results may differ from the reference program's by a relative error of at most 0.0043.
Values may be sent and summed in bfloat16 or wider, within the bound.
A program may use at most 64 MiB of HBM per device.

```python
import jax
import jax.numpy as jnp
from jax import lax

BS = 128
NNZ = 12
MW = 2
M = 4
REACH = 2
ROWS = 3
NCL = 1536


def draw_p_cols(key, part):
    key = jax.random.fold_in(key, 11)
    candidates = (2 * REACH + 1) * ROWS
    row_keys = jax.random.split(key, NCL)
    chosen = jax.vmap(lambda single: jax.random.permutation(single, candidates)[:NNZ])(row_keys)
    device_of = jnp.arange(NCL, dtype=jnp.int32) // ROWS
    columns = (chosen.astype(jnp.int32) + (device_of[:, None] - REACH) * ROWS) % NCL
    return columns.astype(jnp.int32)


def pattern(key, upper):
    live_key, value_key = jax.random.split(key)
    live = jax.random.randint(live_key, (NCL, M, NNZ), 0, 2)
    values = jax.random.randint(value_key, (NCL, M, NNZ), 0, upper)
    return jnp.where(live == 1, values, -1).astype(jnp.int32)


def draw_sel_square(key, part):
    key = jax.random.fold_in(key, 12)
    return pattern(key, MW)


def draw_sel_cube(key, part):
    key = jax.random.fold_in(key, 13)
    return pattern(key, M)


def steps_of(rng, extent, shards, smallest, top_value):
    gain, own = 1.0, jax.random.fold_in(rng, 6)
    for dim, blocks in shards:
        heights = jnp.exp(jax.random.uniform(jax.random.fold_in(own, dim), (blocks,), jnp.float32, smallest / len(shards), top_value / len(shards)))
        gain = gain * jnp.repeat(heights, extent[dim] // blocks).reshape([-1 if axis == dim else 1 for axis in range(len(extent))])
    return gain


def noise(key, extent, spread, reach, cuts=(), kind=jnp.bfloat16):
    loudness = steps_of(key, extent, cuts, -0.22, 0.18) if cuts else 1.0
    values = jax.random.normal(key, extent, jnp.float32) * spread * loudness
    return jnp.minimum(jnp.maximum(values, -reach), reach).astype(kind)


def setup_inputs(seed: int = 0) -> dict:
    arg_keys = jax.random.split(jax.random.key(seed), 5)
    p_blocks = noise(arg_keys[0], (NCL, NNZ, BS, BS), (BS * 5 // 4) ** -0.5, 0.5, ((0, 512),))
    p_cols = draw_p_cols(jax.random.fold_in(arg_keys[4], 71), 0)
    sel_square = draw_sel_square(jax.random.fold_in(arg_keys[4], 71), 0)
    sel_cube = draw_sel_cube(jax.random.fold_in(arg_keys[4], 71), 0)
    return {"p_blocks": p_blocks, "p_cols": p_cols, "sel_square": sel_square, "sel_cube": sel_cube}


def products(p_blocks, p_cols, selection, flattened, per_row):
    def one_row(packed):
        blocks, columns, picked = packed
        position = columns[None, :] * per_row + jnp.maximum(picked, 0)
        operand = jnp.take(flattened, position, axis=0).astype(jnp.float32)
        operand = jnp.where((picked >= 0)[:, :, None, None], operand, jnp.zeros((), jnp.float32))
        return jnp.einsum("axy,sayz->sxz", blocks.astype(jnp.float32), operand)

    return lax.map(one_row, (p_blocks, p_cols, selection))


def reference(p_blocks, p_cols, sel_square, sel_cube):
    flat_window = p_blocks[:, :MW].reshape(NCL * MW, BS, BS)
    square = products(p_blocks, p_cols, sel_square, flat_window, MW)
    square_round = square.astype(jnp.bfloat16)
    cube = products(p_blocks, p_cols, sel_cube, square_round.reshape(NCL * M, BS, BS), M)
    return (3.0 * square - 2.0 * cube).astype(jnp.bfloat16)
```

```python
import functools

import jax
import jax.numpy as jnp
from jax import lax
from jax.experimental import pallas as pl
from jax.experimental.pallas import tpu as pltpu
from jax.sharding import PartitionSpec as P

MW = 2
REACH = 2
SLOTS = 6
RIGHT, LEFT, OPPOSITE, ACROSS, SIDE = range(5)


class Spread:
    def __init__(self, buffer, unit, chunks, send_sem, recv_sem, place):
        self.buffer, self.unit, self.chunks = buffer, unit, chunks
        self.send_sem, self.recv_sem = send_sem, recv_sem
        self.x, self.right, self.left, self.across = place

    def rows(self, slot, k):
        offset, size, _ = self.chunks[k]
        return self.buffer.at[pl.ds(slot * self.unit + offset, size)]

    def copy(self, way, k):
        x = self.x
        opposite = 4 - 4 * (x // 2)
        if way == RIGHT:
            there = lax.rem(x + 1, 4)
            source, target, device = 2, 5 - 4 * ((there + 3) // 4), {"row": self.right}
        elif way == LEFT:
            there = lax.rem(x + 3, 4)
            source, target, device = 2, 3 + 2 * (there // 3), {"row": self.left}
        elif way == OPPOSITE:
            if self.chunks[k][2] == RIGHT:
                there = lax.rem(x + 1, 4)
                source, device = 5 - 4 * ((x + 3) // 4), {"row": self.right}
            else:
                there = lax.rem(x + 3, 4)
                source, device = 3 + 2 * (x // 3), {"row": self.left}
            target = 4 - 4 * (there // 2)
        elif way == ACROSS:
            source, target, device = opposite, 4 - opposite, {"dom": self.across}
        else:
            source, target, device = 5, 1 + 2 * (x // 3), {"dom": self.across}
        return pltpu.make_async_remote_copy(
            src_ref=self.rows(source, k),
            dst_ref=self.rows(target, k),
            send_sem=self.send_sem.at[way, k],
            recv_sem=self.recv_sem.at[way, k],
            device_id=device,
            device_id_type=pl.DeviceIdType.MESH,
        )

    def at_end(self, end, way, k, action):
        @pl.when(self.x == end)
        def _():
            getattr(self.copy(way, k), action)()

    def send(self, part):
        for way in (RIGHT, LEFT):
            for k in part:
                if self.chunks[k][2] == way:
                    self.copy(way, k).start()
        for way in (RIGHT, LEFT):
            for k in part:
                if self.chunks[k][2] != way:
                    self.copy(way, k).start()

    def arrive(self, way, k):
        self.copy(way, k).wait_recv()
        if way == RIGHT:
            self.at_end(0, SIDE, k, "start")
        else:
            self.at_end(3, SIDE, k, "start")

    def pass_on(self):
        every = range(len(self.chunks))
        for k in every:
            way = self.chunks[k][2]
            self.copy(way, k).wait_recv()
            self.copy(OPPOSITE, k).start()
            self.at_end(0 if way == RIGHT else 3, SIDE, k, "start")
        for k in every:
            way = LEFT if self.chunks[k][2] == RIGHT else RIGHT
            self.copy(way, k).wait_recv()
            self.at_end(0 if way == RIGHT else 3, SIDE, k, "start")
        for k in every:
            self.copy(OPPOSITE, k).wait_recv()
            self.copy(ACROSS, k).start()
        for k in every:
            self.at_end(0, SIDE, k, "wait_recv")
            self.at_end(3, SIDE, k, "wait_recv")
        for k in every:
            self.copy(ACROSS, k).wait_recv()

    def finish(self):
        for k in range(len(self.chunks)):
            for way in (RIGHT, LEFT, OPPOSITE, ACROSS):
                self.copy(way, k).wait_send()
            self.at_end(0, SIDE, k, "wait_send")
            self.at_end(3, SIDE, k, "wait_send")


def contract(blocks, nearby, zero, per_row, row, cols_ref, sel_ref, origin, clusters):
    count, products = cols_ref.shape[1], sel_ref.shape[1]
    total = None
    for pair in range(0, count, 2):
        left = jnp.concatenate([blocks[row, pair], blocks[row, pair + 1]], axis=1)
        right = []
        for a in (pair, pair + 1):
            base = lax.rem(cols_ref[row, a] - origin + clusters, clusters) * per_row
            line = []
            for s in range(products):
                picked = sel_ref[row, s, a]
                line.append(nearby[jnp.where(picked >= 0, jnp.minimum(base + picked, zero), zero)])
            right.append(jnp.concatenate(line, axis=1))
        term = jnp.dot(left, jnp.concatenate(right, axis=0), preferred_element_type=jnp.float32)
        total = term if total is None else total + term
    return total


def kernel(
    doms, p_hbm, cols_ref, sel_square_ref, sel_cube_ref, out_ref,
    blocks, window, square, total, local_sem, window_send, window_recv, square_send, square_recv,
):
    rows, products = out_ref.shape[0], out_ref.shape[1]
    size = out_ref.shape[2]
    x, dom = lax.axis_index("row"), lax.axis_index("dom")
    ahead, behind = lax.rem(dom + 1, doms), lax.rem(dom + doms - 1, doms)
    right, left = lax.rem(x + 1, 4), lax.rem(x + 3, 4)
    across = lax.rem(dom + doms + 1 - 2 * (x // 2), doms)
    clusters = doms * 4 * rows
    origin = ((dom * 4 + x) - REACH) * rows

    unit_w, unit_q = rows * MW, rows * products
    loads = [
        pltpu.make_async_copy(
            p_hbm.at[i, pl.ds(0, MW)], window.at[pl.ds(2 * unit_w + i * MW, MW)], local_sem.at[i]
        )
        for i in range(rows)
    ]
    loads.append(pltpu.make_async_copy(p_hbm, blocks, local_sem.at[rows]))
    for load in loads:
        load.start()

    barrier = pltpu.get_barrier_semaphore()
    for device in ({"row": right}, {"row": left}, {"dom": ahead}, {"dom": behind}):
        pl.semaphore_signal(barrier, inc=1, device_id=device, device_id_type=pl.DeviceIdType.MESH)
    zero_w, zero_q = SLOTS * unit_w, SLOTS * unit_q
    window[zero_w] = jnp.zeros((size, size), window.dtype)
    square[zero_q] = jnp.zeros((size, size), square.dtype)
    for load in loads[:rows]:
        load.wait()
    pl.semaphore_wait(barrier, 4)

    place = (x, right, left, across)
    half = unit_w // 2
    chunks = [(k, 1, RIGHT if k < half else LEFT) for k in range(unit_w)]
    first = Spread(window, unit_w, chunks, window_send, window_recv, place)
    pairs = products // 2
    chunks = [(k * pairs, pairs, RIGHT if k % 2 == 0 else LEFT) for k in range(2 * rows)]
    second = Spread(square, unit_q, chunks, square_send, square_recv, place)

    first.send(range(unit_w))
    first.pass_on()
    loads[rows].wait()
    for i in range(rows):
        value = contract(blocks, window, zero_w, MW, i, cols_ref, sel_square_ref, origin, clusters)
        total[i] = value
        for s in range(products):
            square[2 * unit_q + i * products + s] = value[:, s * size:(s + 1) * size].astype(square.dtype)
        second.send((2 * i, 2 * i + 1))
    second.pass_on()
    for i in range(rows):
        value = contract(blocks, square, zero_q, products, i, cols_ref, sel_cube_ref, origin, clusters)
        value = 3.0 * total[i] - 2.0 * value
        for s in range(products):
            out_ref[i, s] = value[:, s * size:(s + 1) * size].astype(out_ref.dtype)
    first.finish()
    second.finish()


def solution(mesh):
    doms, row_devices = mesh.shape["dom"], mesh.shape["row"]
    assert row_devices == 4

    def per_device(p_blocks, p_cols, sel_square, sel_cube):
        rows, count, size, _ = p_blocks.shape
        products = sel_square.shape[1]
        unit_w, unit_q = rows * MW, rows * products
        flops = 2 * 2 * rows * products * count * size**3
        return pl.pallas_call(
            functools.partial(kernel, doms),
            out_shape=jax.ShapeDtypeStruct((rows, products, size, size), jnp.bfloat16),
            in_specs=[pl.BlockSpec(memory_space=pl.ANY)] + [pl.BlockSpec(memory_space=pltpu.SMEM)] * 3,
            out_specs=pl.BlockSpec(memory_space=pltpu.VMEM),
            scratch_shapes=[
                pltpu.VMEM((rows, count, size, size), jnp.bfloat16),
                pltpu.VMEM((SLOTS * unit_w + 1, size, size), jnp.bfloat16),
                pltpu.VMEM((SLOTS * unit_q + 1, size, size), jnp.bfloat16),
                pltpu.VMEM((rows, size, products * size), jnp.float32),
                pltpu.SemaphoreType.DMA((rows + 1,)),
                pltpu.SemaphoreType.DMA((5, unit_w)),
                pltpu.SemaphoreType.DMA((5, unit_w)),
                pltpu.SemaphoreType.DMA((5, 2 * rows)),
                pltpu.SemaphoreType.DMA((5, 2 * rows)),
            ],
            cost_estimate=pl.CostEstimate(flops=flops, bytes_accessed=4 * p_blocks.size, transcendentals=0),
            compiler_params=pltpu.CompilerParams(
                collective_id=0, has_side_effects=True, vmem_limit_bytes=32 * 1024 * 1024
            ),
        )(p_blocks, p_cols, sel_square, sel_cube)

    return jax.shard_map(
        per_device,
        mesh=mesh,
        in_specs=(
            P(("dom", "row"), None, None, None),
            P(("dom", "row"), None),
            P(("dom", "row"), None, None),
            P(("dom", "row"), None, None),
        ),
        out_specs=P(("dom", "row"), None, None, None),
        check_vma=False,
    )
```

```python
import functools

import jax
import jax.numpy as jnp
from jax import lax
from jax.experimental import pallas as pl
from jax.experimental.pallas import tpu as pltpu
from jax.sharding import PartitionSpec as P

MW = 2
REACH = 2
NEAR = 2 * REACH + 1
SLOTS = NEAR + 1
RIGHT, LEFT, OPPOSITE, ACROSS, SIDE = range(5)


class Spread:
    def __init__(self, buffer, chunks, sems, place):
        self.buffer, self.chunks = buffer, chunks
        self.send_sem, self.recv_sem = sems
        self.x, self.right, self.left, self.across, self.spot = place

    def copy(self, way, k):
        x = self.x
        cut, passed = self.chunks[k]
        opposite = 4 - 4 * (x // 2)
        if way == RIGHT:
            there = lax.rem(x + 1, 4)
            source, target, device = 2, 5 - 4 * ((there + 3) // 4), {"row": self.right}
        elif way == LEFT:
            there = lax.rem(x + 3, 4)
            source, target, device = 2, 3 + 2 * (there // 3), {"row": self.left}
        elif way == OPPOSITE:
            if passed == RIGHT:
                there = lax.rem(x + 1, 4)
                source, device = 5 - 4 * ((x + 3) // 4), {"row": self.right}
            else:
                there = lax.rem(x + 3, 4)
                source, device = 3 + 2 * (x // 3), {"row": self.left}
            target = 4 - 4 * (there // 2)
        elif way == ACROSS:
            source, target, device = opposite, 4 - opposite, {"dom": self.across}
        else:
            source, target, device = 5, 1 + 2 * (x // 3), {"dom": self.across}
        return pltpu.make_async_remote_copy(
            src_ref=cut(self.buffer, source),
            dst_ref=cut(self.buffer, target),
            send_sem=self.send_sem.at[way, k],
            recv_sem=self.recv_sem.at[way, k],
            device_id=device,
            device_id_type=pl.DeviceIdType.MESH,
        )

    def at_end(self, end, way, k, action):
        @pl.when(self.x == end)
        def _():
            getattr(self.copy(way, k), action)()

    def part(self, part):
        return range(len(self.chunks)) if part is None else part

    def send_passed(self, part=None):
        for k in self.part(part):
            self.copy(self.chunks[k][1], k).start()

    def send_urgent(self, part=None):
        for spot, way in ((0, LEFT), (7, RIGHT)):
            @pl.when(self.spot == spot)
            def _():
                for k in self.part(part):
                    if self.chunks[k][1] != way:
                        self.copy(way, k).start()

    def send_rest(self, part=None):
        for spot, way in ((0, LEFT), (7, RIGHT)):
            @pl.when(self.spot != spot)
            def _():
                for k in self.part(part):
                    if self.chunks[k][1] != way:
                        self.copy(way, k).start()

    def pass_on(self, part=None):
        for k in self.part(part):
            way = self.chunks[k][1]
            self.copy(way, k).wait_recv()
            self.copy(OPPOSITE, k).start()
            self.at_end(0 if way == RIGHT else 3, SIDE, k, "start")

    def take_rest(self, part=None):
        for k in self.part(part):
            way = LEFT + RIGHT - self.chunks[k][1]
            self.copy(way, k).wait_recv()
            self.at_end(0 if way == RIGHT else 3, SIDE, k, "start")

    def send_across(self, part=None):
        for k in self.part(part):
            self.copy(OPPOSITE, k).wait_recv()
            self.copy(ACROSS, k).start()

    def take_across(self, part=None):
        for k in self.part(part):
            self.at_end(0, SIDE, k, "wait_recv")
            self.at_end(3, SIDE, k, "wait_recv")
            self.copy(ACROSS, k).wait_recv()

    def finish(self):
        for k in range(len(self.chunks)):
            for way in (RIGHT, LEFT, OPPOSITE, ACROSS):
                self.copy(way, k).wait_send()
            self.at_end(0, SIDE, k, "wait_send")
            self.at_end(3, SIDE, k, "wait_send")


def swapped(tile):
    half = tile.shape[1] // 2
    return jnp.concatenate([tile[:, half:], tile[:, :half]], axis=1)


def joined(first, second):
    half = first.shape[1] // 2
    return jnp.concatenate([first[:, :half], second[:, half:]], axis=1)


def place_picks(places, cols_ref, sel_ref, tiles, zero, origin, clusters, reach_rows):
    rows, products, count = sel_ref.shape
    turned = zero + 1

    def one(a, carry):
        for i in range(rows):
            near = cols_ref[i, a] - origin
            near = jnp.where(near < 0, near + clusters, near)
            near = jnp.where(near >= clusters, near - clusters, near)
            base = jnp.minimum(near, reach_rows - 1) * tiles
            for s in range(products):
                picked = sel_ref[i, s, a]
                odd = lax.bitwise_and(picked, 1)
                turn = odd if s % 2 == 0 else 1 - odd
                tile = base + lax.shift_right_arithmetic(picked, 1) + turned * turn
                places[(i * count + a) * products + s] = jnp.where(picked >= 0, tile, zero)
        return carry

    lax.fori_loop(0, count, one, 0)


def contract(blocks, nearby, places, row, products):
    count = blocks.shape[1]
    total = None
    for pair in range(0, count, 2):
        left = jnp.concatenate([blocks[row, pair], blocks[row, pair + 1]], axis=1)
        right = []
        for a in (pair, pair + 1):
            at = (row * count + a) * products
            line = [joined(nearby[places[at + s]], nearby[places[at + s + 1]]) for s in range(0, products, 2)]
            right.append(jnp.concatenate(line, axis=1))
        term = jnp.dot(left, jnp.concatenate(right, axis=0), preferred_element_type=jnp.float32)
        total = term if total is None else total + term
    return total


def kernel(
    doms, p_hbm, cols_hbm, sel_square_hbm, sel_cube_hbm, out_ref,
    blocks, cols_ref, sel_square_ref, sel_cube_ref, window_places, square_places, window0, window1, square0, square1, total, first_out,
    local_sem, window_send, window_recv, square_send, square_recv,
):
    rows, products, size = out_ref.shape[:3]
    half = size // 2
    x, dom = lax.axis_index("row"), lax.axis_index("dom")
    ahead, behind = lax.rem(dom + 1, doms), lax.rem(dom + doms - 1, doms)
    right, left = lax.rem(x + 1, 4), lax.rem(x + 3, 4)
    across = lax.rem(dom + doms + 1 - 2 * (x // 2), doms)
    clusters = doms * 4 * rows
    origin = ((dom * 4 + x) - REACH) * rows
    reach_rows = NEAR * rows

    own = pltpu.make_async_copy(p_hbm.at[:, pl.ds(0, MW)], blocks.at[:, pl.ds(0, MW)], local_sem.at[0])
    rest = blocks.shape[1] - MW
    others = [
        pltpu.make_async_copy(p_hbm.at[:, pl.ds(MW, rest)], blocks.at[:, pl.ds(MW, rest)], local_sem.at[1]),
        pltpu.make_async_copy(cols_hbm, cols_ref, local_sem.at[2]),
        pltpu.make_async_copy(sel_square_hbm, sel_square_ref, local_sem.at[3]),
        pltpu.make_async_copy(sel_cube_hbm, sel_cube_ref, local_sem.at[4]),
    ]
    own.start()
    for load in others:
        load.start()

    barrier = pltpu.get_barrier_semaphore()
    for device in ({"row": right}, {"row": left}, {"dom": ahead}, {"dom": behind}):
        pl.semaphore_signal(barrier, inc=1, device_id=device, device_id_type=pl.DeviceIdType.MESH)

    tiles = products // 2
    zero_w, zero_q = SLOTS * rows, SLOTS * rows * tiles
    windows, squares = (window0, window1), (square0, square1)
    for buffer, zero in ((window0, zero_w), (window1, zero_w), (square0, zero_q), (square1, zero_q)):
        buffer[zero] = jnp.zeros((size, size), buffer.dtype)
    own.wait()
    for i in range(rows):
        one, two = blocks[i, 0], blocks[i, 1]
        window0[REACH * rows + i] = joined(one, swapped(two))
        window1[REACH * rows + i] = joined(swapped(one), two)

    place = (x, right, left, across, x + 4 * lax.rem(dom, 2))

    def window_cut(tile, part):
        return lambda buffer, slot: buffer.at[slot * rows + tile, pl.ds(part * half, half)]

    def square_cut(tile):
        return lambda buffer, slot: buffer.at[slot * rows * tiles + tile]

    window_chunks = [(window_cut(tile, part), (RIGHT, LEFT)[part]) for tile in range(rows) for part in (0, 1)]
    square_chunks = [(square_cut(tile), RIGHT if tile % 2 == 0 else LEFT) for tile in range(rows * tiles)]
    w0, w1 = (Spread(windows[h], window_chunks, (window_send.at[h], window_recv.at[h]), place) for h in (0, 1))
    q0, q1 = (Spread(squares[h], square_chunks, (square_send.at[h], square_recv.at[h]), place) for h in (0, 1))

    def turn(buffer, tiles, zero):
        for tile in range(reach_rows * tiles):
            buffer[zero + 1 + tile] = swapped(buffer[tile])

    def make_square(h, spread):
        turn(windows[h], 1, zero_w)
        for i in range(rows):
            value = contract(blocks, windows[h], window_places, i, products)
            total[h, i] = value
            for t in range(tiles):
                squares[h][(REACH * rows + i) * tiles + t] = value[:, t * size:(t + 1) * size].astype(jnp.bfloat16)
            part = range(i * tiles, (i + 1) * tiles)
            spread.send_passed(part)
        spread.send_urgent()

    def purified(h, i):
        value = contract(blocks, squares[h], square_places, i, products)
        return (3.0 * total[h, i] - 2.0 * value).astype(out_ref.dtype)

    pl.semaphore_wait(barrier, 4)
    w0.send_passed()
    w0.send_urgent()
    w0.send_rest((0, 1))
    w0.pass_on((0, 1))
    w0.send_rest((2, 3))
    w0.pass_on((2, 3))
    w0.send_rest((4, 5))
    w0.pass_on((4, 5))
    w1.send_passed()
    w1.send_urgent()
    for load in others:
        load.wait()
    place_picks(window_places, cols_ref, sel_square_ref, 1, zero_w, origin, clusters, reach_rows)
    w0.take_rest()
    w0.send_across()
    w1.pass_on()
    w1.send_rest()
    place_picks(square_places, cols_ref, sel_cube_ref, tiles, zero_q, origin, clusters, reach_rows)
    w0.take_across()
    make_square(0, q0)
    w1.take_rest()
    w1.send_across()
    q0.pass_on()
    q0.send_rest()
    w1.take_across()
    make_square(1, q1)
    q0.take_rest()
    q0.send_across()
    q1.pass_on()
    q1.send_rest()
    q0.take_across()
    turn(square0, tiles, zero_q)
    for i in range(rows):
        first_out[i] = purified(0, i)
    q1.send_across()
    q1.take_rest()
    q1.take_across()
    turn(square1, tiles, zero_q)
    for i in range(rows):
        early, late = first_out[i], purified(1, i)
        for t in range(tiles):
            one, two = early[:, t * size:(t + 1) * size], late[:, t * size:(t + 1) * size]
            out_ref[i, 2 * t] = joined(one, swapped(two))
            out_ref[i, 2 * t + 1] = joined(swapped(one), two)
    for spread in (w0, w1, q0, q1):
        spread.finish()


def solution(mesh):
    doms, row_devices = mesh.shape["dom"], mesh.shape["row"]
    assert row_devices == 4

    def per_device(p_blocks, p_cols, sel_square, sel_cube):
        rows, count, size, _ = p_blocks.shape
        products = sel_square.shape[1]
        tiles = products // 2
        flops = 2 * 2 * rows * products * count * size**3
        window_tiles = (SLOTS + NEAR) * rows + 1
        square_tiles = (SLOTS + NEAR) * rows * tiles + 1
        return pl.pallas_call(
            functools.partial(kernel, doms),
            out_shape=jax.ShapeDtypeStruct((rows, products, size, size), jnp.bfloat16),
            in_specs=[pl.BlockSpec(memory_space=pltpu.HBM)] * 4,
            out_specs=pl.BlockSpec(memory_space=pltpu.VMEM),
            scratch_shapes=[
                pltpu.VMEM((rows, count, size, size), jnp.bfloat16),
                pltpu.SMEM(p_cols.shape, jnp.int32),
                pltpu.SMEM(sel_square.shape, jnp.int32),
                pltpu.SMEM(sel_cube.shape, jnp.int32),
                pltpu.SMEM((rows * count * products,), jnp.int32),
                pltpu.SMEM((rows * count * products,), jnp.int32),
                pltpu.VMEM((window_tiles, size, size), jnp.bfloat16),
                pltpu.VMEM((window_tiles, size, size), jnp.bfloat16),
                pltpu.VMEM((square_tiles, size, size), jnp.bfloat16),
                pltpu.VMEM((square_tiles, size, size), jnp.bfloat16),
                pltpu.VMEM((2, rows, size, tiles * size), jnp.float32),
                pltpu.VMEM((rows, size, tiles * size), jnp.bfloat16),
                pltpu.SemaphoreType.DMA((5,)),
                pltpu.SemaphoreType.DMA((2, 5, 2 * rows)),
                pltpu.SemaphoreType.DMA((2, 5, 2 * rows)),
                pltpu.SemaphoreType.DMA((2, 5, rows * tiles)),
                pltpu.SemaphoreType.DMA((2, 5, rows * tiles)),
            ],
            cost_estimate=pl.CostEstimate(flops=flops, bytes_accessed=4 * p_blocks.size, transcendentals=0),
            compiler_params=pltpu.CompilerParams(
                collective_id=0, has_side_effects=True, vmem_limit_bytes=60 * 1024 * 1024
            ),
        )(p_blocks, p_cols, sel_square, sel_cube)

    return jax.shard_map(
        per_device,
        mesh=mesh,
        in_specs=(
            P(("dom", "row"), None, None, None),
            P(("dom", "row"), None),
            P(("dom", "row"), None, None),
            P(("dom", "row"), None, None),
        ),
        out_specs=P(("dom", "row"), None, None, None),
        check_vma=False,
    )
```

```python
import functools

import jax
import jax.numpy as jnp
from jax import lax
from jax.experimental import pallas as pl
from jax.experimental.pallas import tpu as pltpu
from jax.sharding import PartitionSpec as P

MW = 2
REACH = 2
NEAR = 2 * REACH + 1
SLOTS = NEAR + 1
RIGHT, LEFT, OPPOSITE, ACROSS, SIDE = range(5)


class Spread:
    def __init__(self, buffer, chunks, sems, place):
        self.buffer, self.chunks = buffer, chunks
        self.send_sem, self.recv_sem = sems
        self.x, self.right, self.left, self.across, self.spot = place

    def copy(self, way, k):
        x = self.x
        cut, passed = self.chunks[k]
        opposite = 4 - 4 * (x // 2)
        if way == RIGHT:
            there = lax.rem(x + 1, 4)
            source, target, device = 2, 5 - 4 * ((there + 3) // 4), {"row": self.right}
        elif way == LEFT:
            there = lax.rem(x + 3, 4)
            source, target, device = 2, 3 + 2 * (there // 3), {"row": self.left}
        elif way == OPPOSITE:
            if passed == RIGHT:
                there = lax.rem(x + 1, 4)
                source, device = 5 - 4 * ((x + 3) // 4), {"row": self.right}
            else:
                there = lax.rem(x + 3, 4)
                source, device = 3 + 2 * (x // 3), {"row": self.left}
            target = 4 - 4 * (there // 2)
        elif way == ACROSS:
            source, target, device = opposite, 4 - opposite, {"dom": self.across}
        else:
            source, target, device = 5, 1 + 2 * (x // 3), {"dom": self.across}
        return pltpu.make_async_remote_copy(
            src_ref=cut(self.buffer, source),
            dst_ref=cut(self.buffer, target),
            send_sem=self.send_sem.at[way, k],
            recv_sem=self.recv_sem.at[way, k],
            device_id=device,
            device_id_type=pl.DeviceIdType.MESH,
        )

    def at_end(self, end, way, k, action):
        @pl.when(self.x == end)
        def _():
            getattr(self.copy(way, k), action)()

    def part(self, part):
        return range(len(self.chunks)) if part is None else part

    def send_passed(self, part=None):
        for k in self.part(part):
            self.copy(self.chunks[k][1], k).start()

    def send_urgent(self, part=None):
        for spot, way in ((0, LEFT), (7, RIGHT)):
            @pl.when(self.spot == spot)
            def _():
                for k in self.part(part):
                    if self.chunks[k][1] != way:
                        self.copy(way, k).start()

    def send_rest(self, part=None):
        for spot, way in ((0, LEFT), (7, RIGHT)):
            @pl.when(self.spot != spot)
            def _():
                for k in self.part(part):
                    if self.chunks[k][1] != way:
                        self.copy(way, k).start()

    def pass_on(self, part=None, sides=True):
        for k in self.part(part):
            self.copy(self.chunks[k][1], k).wait_recv()
            self.copy(OPPOSITE, k).start()
            if sides:
                self.send_sides((k,))

    def send_sides(self, part=None):
        for k in self.part(part):
            self.at_end(0 if self.chunks[k][1] == RIGHT else 3, SIDE, k, "start")

    def take_rest(self, part=None):
        for k in self.part(part):
            way = LEFT + RIGHT - self.chunks[k][1]
            self.copy(way, k).wait_recv()
            self.at_end(0 if way == RIGHT else 3, SIDE, k, "start")

    def send_across(self, part=None):
        for k in self.part(part):
            self.copy(OPPOSITE, k).wait_recv()
            self.copy(ACROSS, k).start()

    def take_across(self, part=None):
        for k in self.part(part):
            self.at_end(0, SIDE, k, "wait_recv")
            self.at_end(3, SIDE, k, "wait_recv")
            self.copy(ACROSS, k).wait_recv()

    def finish(self):
        for k in range(len(self.chunks)):
            for way in (RIGHT, LEFT, OPPOSITE, ACROSS):
                self.copy(way, k).wait_send()
            self.at_end(0, SIDE, k, "wait_send")
            self.at_end(3, SIDE, k, "wait_send")


def swapped(tile):
    half = tile.shape[1] // 2
    return jnp.concatenate([tile[:, half:], tile[:, :half]], axis=1)


def joined(first, second):
    half = first.shape[1] // 2
    return jnp.concatenate([first[:, :half], second[:, half:]], axis=1)


def place_picks(places, cols_ref, sel_ref, tiles, zero, origin, clusters, reach_rows):
    rows, products, count = sel_ref.shape
    turned = zero + 1

    def one(a, carry):
        for i in range(rows):
            near = cols_ref[i, a] - origin
            near = jnp.where(near < 0, near + clusters, near)
            near = jnp.where(near >= clusters, near - clusters, near)
            base = jnp.minimum(near, reach_rows - 1) * tiles
            for s in range(products):
                picked = sel_ref[i, s, a]
                odd = lax.bitwise_and(picked, 1)
                turn = odd if s % 2 == 0 else 1 - odd
                tile = base + lax.shift_right_arithmetic(picked, 1) + turned * turn
                places[(i * count + a) * products + s] = jnp.where(picked >= 0, tile, zero)
        return carry

    lax.fori_loop(0, count, one, 0)


def contract(blocks, nearby, places, row, products):
    count = blocks.shape[1]
    total = None
    for pair in range(0, count, 2):
        left = jnp.concatenate([blocks[row, pair], blocks[row, pair + 1]], axis=1)
        right = []
        for a in (pair, pair + 1):
            at = (row * count + a) * products
            line = [joined(nearby[places[at + s]], nearby[places[at + s + 1]]) for s in range(0, products, 2)]
            right.append(jnp.concatenate(line, axis=1))
        term = jnp.dot(left, jnp.concatenate(right, axis=0), preferred_element_type=jnp.float32)
        total = term if total is None else total + term
    return total


def kernel(
    doms, p_hbm, cols_hbm, sel_square_hbm, sel_cube_hbm, out_ref,
    blocks, cols_ref, sel_square_ref, sel_cube_ref, window_places, square_places, window0, window1, square0, square1, total, first_out,
    local_sem, go_sem, window_send, window_recv, square_send, square_recv,
):
    rows, products, size = out_ref.shape[:3]
    half = size // 2
    x, dom = lax.axis_index("row"), lax.axis_index("dom")
    ahead, behind = lax.rem(dom + 1, doms), lax.rem(dom + doms - 1, doms)
    right, left = lax.rem(x + 1, 4), lax.rem(x + 3, 4)
    across = lax.rem(dom + doms + 1 - 2 * (x // 2), doms)
    clusters = doms * 4 * rows
    origin = ((dom * 4 + x) - REACH) * rows
    reach_rows = NEAR * rows

    own = pltpu.make_async_copy(p_hbm.at[:, pl.ds(0, MW)], blocks.at[:, pl.ds(0, MW)], local_sem.at[0])
    rest = blocks.shape[1] - MW
    others = [
        pltpu.make_async_copy(p_hbm.at[:, pl.ds(MW, rest)], blocks.at[:, pl.ds(MW, rest)], local_sem.at[1]),
        pltpu.make_async_copy(cols_hbm, cols_ref, local_sem.at[2]),
        pltpu.make_async_copy(sel_square_hbm, sel_square_ref, local_sem.at[3]),
        pltpu.make_async_copy(sel_cube_hbm, sel_cube_ref, local_sem.at[4]),
    ]
    own.start()
    for load in others:
        load.start()

    barrier = pltpu.get_barrier_semaphore()
    for device in ({"row": right}, {"row": left}, {"dom": behind}):
        pl.semaphore_signal(barrier, inc=1, device_id=device, device_id_type=pl.DeviceIdType.MESH)

    tiles = products // 2
    zero_w, zero_q = SLOTS * rows, SLOTS * rows * tiles
    windows, squares = (window0, window1), (square0, square1)
    for buffer, zero in ((window0, zero_w), (window1, zero_w), (square0, zero_q), (square1, zero_q)):
        buffer[zero] = jnp.zeros((size, size), buffer.dtype)
    own.wait()
    for i in range(rows):
        one, two = blocks[i, 0], blocks[i, 1]
        window0[REACH * rows + i] = joined(one, swapped(two))
        window1[REACH * rows + i] = joined(swapped(one), two)

    place = (x, right, left, across, x + 4 * lax.rem(dom, 2))

    def window_cut(tile, part):
        return lambda buffer, slot: buffer.at[slot * rows + tile, pl.ds(part * half, half)]

    def square_cut(tile):
        return lambda buffer, slot: buffer.at[slot * rows * tiles + tile]

    window_chunks = [(window_cut(tile, part), (RIGHT, LEFT)[part]) for tile in range(rows) for part in (0, 1)]
    square_chunks = [(square_cut(tile), RIGHT if tile % 2 == 0 else LEFT) for tile in range(rows * tiles)]
    w0, w1 = (Spread(windows[h], window_chunks, (window_send.at[h], window_recv.at[h]), place) for h in (0, 1))
    q0, q1 = (Spread(squares[h], square_chunks, (square_send.at[h], square_recv.at[h]), place) for h in (0, 1))

    def turn(buffer, tiles, zero):
        for tile in range(reach_rows * tiles):
            buffer[zero + 1 + tile] = swapped(buffer[tile])

    def make_square(h, spread):
        turn(windows[h], 1, zero_w)
        for i in range(rows):
            value = contract(blocks, windows[h], window_places, i, products)
            total[h, i] = value
            for t in range(tiles):
                squares[h][(REACH * rows + i) * tiles + t] = value[:, t * size:(t + 1) * size].astype(jnp.bfloat16)
            part = range(i * tiles, (i + 1) * tiles)
            spread.send_passed(part)
        spread.send_urgent()

    def purified(h, i):
        value = contract(blocks, squares[h], square_places, i, products)
        return (3.0 * total[h, i] - 2.0 * value).astype(out_ref.dtype)

    pl.semaphore_wait(barrier, 3)

    @pl.when(x >= 2)
    def _():
        pl.semaphore_signal(go_sem, inc=1, device_id={"dom": ahead}, device_id_type=pl.DeviceIdType.MESH)

    w0.send_passed()
    w0.send_urgent()
    w0.send_rest((0, 1))
    w0.pass_on((0, 1), False)
    w0.send_rest((2, 3))
    w0.pass_on((2, 3), False)
    w0.send_rest((4, 5))
    w0.pass_on((4, 5), False)
    w1.send_passed()
    w1.send_urgent()
    for load in others:
        load.wait()
    place_picks(window_places, cols_ref, sel_square_ref, 1, zero_w, origin, clusters, reach_rows)

    @pl.when(x >= 2)
    def _():
        pl.semaphore_wait(go_sem, 1)

    w0.send_sides()
    w0.take_rest()
    w0.send_across()
    w1.pass_on()
    w1.send_rest()
    place_picks(square_places, cols_ref, sel_cube_ref, tiles, zero_q, origin, clusters, reach_rows)
    w0.take_across()
    make_square(0, q0)
    w1.take_rest()
    w1.send_across()
    q0.pass_on()
    q0.send_rest()
    w1.take_across()
    make_square(1, q1)
    q0.take_rest()
    q0.send_across()
    q1.pass_on()
    q1.send_rest()
    q0.take_across()
    turn(square0, tiles, zero_q)
    for i in range(rows):
        first_out[i] = purified(0, i)
    q1.send_across()
    q1.take_rest()
    q1.take_across()
    turn(square1, tiles, zero_q)
    for i in range(rows):
        early, late = first_out[i], purified(1, i)
        for t in range(tiles):
            one, two = early[:, t * size:(t + 1) * size], late[:, t * size:(t + 1) * size]
            out_ref[i, 2 * t] = joined(one, swapped(two))
            out_ref[i, 2 * t + 1] = joined(swapped(one), two)
    for spread in (w0, w1, q0, q1):
        spread.finish()


def solution(mesh):
    doms, row_devices = mesh.shape["dom"], mesh.shape["row"]
    assert row_devices == 4

    def per_device(p_blocks, p_cols, sel_square, sel_cube):
        rows, count, size, _ = p_blocks.shape
        products = sel_square.shape[1]
        tiles = products // 2
        flops = 2 * 2 * rows * products * count * size**3
        window_tiles = (SLOTS + NEAR) * rows + 1
        square_tiles = (SLOTS + NEAR) * rows * tiles + 1
        return pl.pallas_call(
            functools.partial(kernel, doms),
            out_shape=jax.ShapeDtypeStruct((rows, products, size, size), jnp.bfloat16),
            in_specs=[pl.BlockSpec(memory_space=pltpu.HBM)] * 4,
            out_specs=pl.BlockSpec(memory_space=pltpu.VMEM),
            scratch_shapes=[
                pltpu.VMEM((rows, count, size, size), jnp.bfloat16),
                pltpu.SMEM(p_cols.shape, jnp.int32),
                pltpu.SMEM(sel_square.shape, jnp.int32),
                pltpu.SMEM(sel_cube.shape, jnp.int32),
                pltpu.SMEM((rows * count * products,), jnp.int32),
                pltpu.SMEM((rows * count * products,), jnp.int32),
                pltpu.VMEM((window_tiles, size, size), jnp.bfloat16),
                pltpu.VMEM((window_tiles, size, size), jnp.bfloat16),
                pltpu.VMEM((square_tiles, size, size), jnp.bfloat16),
                pltpu.VMEM((square_tiles, size, size), jnp.bfloat16),
                pltpu.VMEM((2, rows, size, tiles * size), jnp.float32),
                pltpu.VMEM((rows, size, tiles * size), jnp.bfloat16),
                pltpu.SemaphoreType.DMA((5,)),
                pltpu.SemaphoreType.REGULAR,
                pltpu.SemaphoreType.DMA((2, 5, 2 * rows)),
                pltpu.SemaphoreType.DMA((2, 5, 2 * rows)),
                pltpu.SemaphoreType.DMA((2, 5, rows * tiles)),
                pltpu.SemaphoreType.DMA((2, 5, rows * tiles)),
            ],
            cost_estimate=pl.CostEstimate(flops=flops, bytes_accessed=4 * p_blocks.size, transcendentals=0),
            compiler_params=pltpu.CompilerParams(
                collective_id=0, has_side_effects=True, vmem_limit_bytes=60 * 1024 * 1024
            ),
        )(p_blocks, p_cols, sel_square, sel_cube)

    return jax.shard_map(
        per_device,
        mesh=mesh,
        in_specs=(
            P(("dom", "row"), None, None, None),
            P(("dom", "row"), None),
            P(("dom", "row"), None, None),
            P(("dom", "row"), None, None),
        ),
        out_specs=P(("dom", "row"), None, None, None),
        check_vma=False,
    )
```

```python
import functools

import jax
import jax.numpy as jnp
from jax import lax
from jax.experimental import pallas as pl
from jax.experimental.pallas import tpu as pltpu
from jax.sharding import PartitionSpec as P

MW = 2
REACH = 2
NEAR = 2 * REACH + 1
SLOTS = NEAR + 1
RIGHT, LEFT, OPPOSITE, ACROSS, SIDE = range(5)


class Spread:
    def __init__(self, buffer, chunks, sems, place):
        self.buffer, self.chunks = buffer, chunks
        self.send_sem, self.recv_sem = sems
        self.x, self.right, self.left, self.across, self.spot = place

    def copy(self, way, k):
        x = self.x
        cut, passed = self.chunks[k]
        opposite = 4 - 4 * (x // 2)
        if way == RIGHT:
            there = lax.rem(x + 1, 4)
            source, target, device = 2, 5 - 4 * ((there + 3) // 4), {"row": self.right}
        elif way == LEFT:
            there = lax.rem(x + 3, 4)
            source, target, device = 2, 3 + 2 * (there // 3), {"row": self.left}
        elif way == OPPOSITE:
            if passed == RIGHT:
                there = lax.rem(x + 1, 4)
                source, device = 5 - 4 * ((x + 3) // 4), {"row": self.right}
            else:
                there = lax.rem(x + 3, 4)
                source, device = 3 + 2 * (x // 3), {"row": self.left}
            target = 4 - 4 * (there // 2)
        elif way == ACROSS:
            source, target, device = opposite, 4 - opposite, {"dom": self.across}
        else:
            source, target, device = 5, 1 + 2 * (x // 3), {"dom": self.across}
        return pltpu.make_async_remote_copy(
            src_ref=cut(self.buffer, source),
            dst_ref=cut(self.buffer, target),
            send_sem=self.send_sem.at[way, k],
            recv_sem=self.recv_sem.at[way, k],
            device_id=device,
            device_id_type=pl.DeviceIdType.MESH,
        )

    def at_end(self, end, way, k, action):
        @pl.when(self.x == end)
        def _():
            getattr(self.copy(way, k), action)()

    def part(self, part):
        return range(len(self.chunks)) if part is None else part

    def send_passed(self, part=None):
        for k in self.part(part):
            self.copy(self.chunks[k][1], k).start()

    def send_urgent(self, part=None):
        for spot, way in ((0, LEFT), (7, RIGHT)):
            @pl.when(self.spot == spot)
            def _():
                for k in self.part(part):
                    if self.chunks[k][1] != way:
                        self.copy(way, k).start()

    def send_rest(self, part=None):
        for spot, way in ((0, LEFT), (7, RIGHT)):
            @pl.when(self.spot != spot)
            def _():
                for k in self.part(part):
                    if self.chunks[k][1] != way:
                        self.copy(way, k).start()

    def pass_on(self, part=None, sides=True):
        for k in self.part(part):
            self.copy(self.chunks[k][1], k).wait_recv()
            self.copy(OPPOSITE, k).start()
            if sides:
                self.send_sides((k,))

    def send_sides(self, part=None):
        for k in self.part(part):
            self.at_end(0 if self.chunks[k][1] == RIGHT else 3, SIDE, k, "start")

    def take_rest(self, part=None):
        for k in self.part(part):
            way = LEFT + RIGHT - self.chunks[k][1]
            self.copy(way, k).wait_recv()
            self.at_end(0 if way == RIGHT else 3, SIDE, k, "start")

    def send_across(self, part=None):
        for k in self.part(part):
            self.copy(OPPOSITE, k).wait_recv()
            self.copy(ACROSS, k).start()

    def take_across(self, part=None):
        for k in self.part(part):
            self.at_end(0, SIDE, k, "wait_recv")
            self.at_end(3, SIDE, k, "wait_recv")
            self.copy(ACROSS, k).wait_recv()

    def finish(self):
        for k in range(len(self.chunks)):
            for way in (RIGHT, LEFT, OPPOSITE, ACROSS):
                self.copy(way, k).wait_send()
            self.at_end(0, SIDE, k, "wait_send")
            self.at_end(3, SIDE, k, "wait_send")


def swapped(tile):
    half = tile.shape[1] // 2
    return jnp.concatenate([tile[:, half:], tile[:, :half]], axis=1)


def joined(first, second):
    half = first.shape[1] // 2
    return jnp.concatenate([first[:, :half], second[:, half:]], axis=1)


def place_picks(places, cols_ref, sel_ref, tiles, zero, origin, clusters, reach_rows):
    rows, products, count = sel_ref.shape
    turned = zero + 1

    def one(a, carry):
        for i in range(rows):
            near = cols_ref[i, a] - origin
            near = jnp.where(near < 0, near + clusters, near)
            near = jnp.where(near >= clusters, near - clusters, near)
            base = jnp.minimum(near, reach_rows - 1) * tiles
            for s in range(products):
                picked = sel_ref[i, s, a]
                odd = lax.bitwise_and(picked, 1)
                turn = odd if s % 2 == 0 else 1 - odd
                tile = base + lax.shift_right_arithmetic(picked, 1) + turned * turn
                places[(i * count + a) * products + s] = jnp.where(picked >= 0, tile, zero)
        return carry

    lax.fori_loop(0, count, one, 0)


def contract(blocks, nearby, places, row, products):
    count = blocks.shape[1]
    total = None
    for pair in range(0, count, 2):
        left = jnp.concatenate([blocks[row, pair], blocks[row, pair + 1]], axis=1)
        right = []
        for a in (pair, pair + 1):
            at = (row * count + a) * products
            line = [joined(nearby[places[at + s]], nearby[places[at + s + 1]]) for s in range(0, products, 2)]
            right.append(jnp.concatenate(line, axis=1))
        term = jnp.dot(left, jnp.concatenate(right, axis=0), preferred_element_type=jnp.float32)
        total = term if total is None else total + term
    return total


def kernel(
    doms, p_hbm, cols_hbm, sel_square_hbm, sel_cube_hbm, out_hbm,
    blocks, cols_ref, sel_square_ref, sel_cube_ref, window_places, square_places, window0, window1, square0, square1, total, first_out, out_ref,
    local_sem, out_sem, go_sem, window_send, window_recv, square_send, square_recv,
):
    rows, products, size = out_ref.shape[:3]
    half = size // 2
    x, dom = lax.axis_index("row"), lax.axis_index("dom")
    ahead, behind = lax.rem(dom + 1, doms), lax.rem(dom + doms - 1, doms)
    right, left = lax.rem(x + 1, 4), lax.rem(x + 3, 4)
    across = lax.rem(dom + doms + 1 - 2 * (x // 2), doms)
    clusters = doms * 4 * rows
    origin = ((dom * 4 + x) - REACH) * rows
    reach_rows = NEAR * rows

    own = pltpu.make_async_copy(p_hbm.at[:, pl.ds(0, MW)], blocks.at[:, pl.ds(0, MW)], local_sem.at[0])
    rest = blocks.shape[1] - MW
    others = [
        pltpu.make_async_copy(p_hbm.at[:, pl.ds(MW, rest)], blocks.at[:, pl.ds(MW, rest)], local_sem.at[1]),
        pltpu.make_async_copy(cols_hbm, cols_ref, local_sem.at[2]),
        pltpu.make_async_copy(sel_square_hbm, sel_square_ref, local_sem.at[3]),
        pltpu.make_async_copy(sel_cube_hbm, sel_cube_ref, local_sem.at[4]),
    ]
    own.start()
    for load in others:
        load.start()

    barrier = pltpu.get_barrier_semaphore()
    for device in ({"row": right}, {"row": left}, {"dom": behind}):
        pl.semaphore_signal(barrier, inc=1, device_id=device, device_id_type=pl.DeviceIdType.MESH)

    tiles = products // 2
    zero_w, zero_q = SLOTS * rows, SLOTS * rows * tiles
    windows, squares = (window0, window1), (square0, square1)
    for buffer, zero in ((window0, zero_w), (window1, zero_w), (square0, zero_q), (square1, zero_q)):
        buffer[zero] = jnp.zeros((size, size), buffer.dtype)
    own.wait()
    for i in range(rows):
        one, two = blocks[i, 0], blocks[i, 1]
        window0[REACH * rows + i] = joined(one, swapped(two))
        window1[REACH * rows + i] = joined(swapped(one), two)

    place = (x, right, left, across, x + 4 * lax.rem(dom, 2))

    def window_cut(tile, part):
        return lambda buffer, slot: buffer.at[slot * rows + tile, pl.ds(part * half, half)]

    def square_cut(tile):
        return lambda buffer, slot: buffer.at[slot * rows * tiles + tile]

    window_chunks = [(window_cut(tile, part), (RIGHT, LEFT)[part]) for tile in range(rows) for part in (0, 1)]
    square_chunks = [(square_cut(tile), RIGHT if tile % 2 == 0 else LEFT) for tile in range(rows * tiles)]
    w0, w1 = (Spread(windows[h], window_chunks, (window_send.at[h], window_recv.at[h]), place) for h in (0, 1))
    q0, q1 = (Spread(squares[h], square_chunks, (square_send.at[h], square_recv.at[h]), place) for h in (0, 1))

    def turn(buffer, unit, zero, slots):
        for slot in slots:
            for tile in range(unit):
                buffer[zero + 1 + slot * unit + tile] = swapped(buffer[slot * unit + tile])

    sooner = (2, 5 - 4 * ((x + 3) // 4), 3 + 2 * (x // 3), 4 - 4 * (x // 2))
    later = (4 * (x // 2), 1 + 2 * (x // 3))

    def make_square(h, spread):
        turn(windows[h], rows, zero_w, later)
        for i in range(rows):
            value = contract(blocks, windows[h], window_places, i, products)
            total[h, i] = value
            for t in range(tiles):
                squares[h][(REACH * rows + i) * tiles + t] = value[:, t * size:(t + 1) * size].astype(jnp.bfloat16)
            part = range(i * tiles, (i + 1) * tiles)
            spread.send_passed(part)
        spread.send_urgent()

    def purified(h, i):
        value = contract(blocks, squares[h], square_places, i, products)
        return (3.0 * total[h, i] - 2.0 * value).astype(out_ref.dtype)

    pl.semaphore_wait(barrier, 3)

    @pl.when(x >= 2)
    def _():
        pl.semaphore_signal(go_sem, inc=1, device_id={"dom": ahead}, device_id_type=pl.DeviceIdType.MESH)

    w0.send_passed()
    w0.send_urgent()
    w0.send_rest((0, 1))
    w0.pass_on((0, 1), False)
    w0.send_rest((2, 3))
    w0.pass_on((2, 3), False)
    w0.send_rest((4, 5))
    w0.pass_on((4, 5), False)
    w1.send_passed()
    w1.send_urgent()
    for load in others:
        load.wait()
    place_picks(window_places, cols_ref, sel_square_ref, 1, zero_w, origin, clusters, reach_rows)

    @pl.when(x >= 2)
    def _():
        pl.semaphore_wait(go_sem, 1)

    w0.send_sides()
    w0.take_rest()
    w0.send_across()
    w1.pass_on()
    w1.send_rest()
    place_picks(square_places, cols_ref, sel_cube_ref, tiles, zero_q, origin, clusters, reach_rows)
    turn(window0, rows, zero_w, sooner)
    w0.take_across()
    make_square(0, q0)
    w1.take_rest()
    w1.send_across()
    q0.pass_on()
    q0.send_rest()
    turn(window1, rows, zero_w, sooner)
    w1.take_across()
    make_square(1, q1)
    q0.send_across()
    q0.take_rest()
    q1.pass_on()
    q1.send_rest()
    q0.take_across()
    turn(square0, rows * tiles, zero_q, sooner + later)
    for i in range(rows):
        first_out[i] = purified(0, i)
    q1.send_across()
    q1.take_rest()
    turn(square1, rows * tiles, zero_q, sooner)
    q1.take_across()
    turn(square1, rows * tiles, zero_q, later)
    for i in range(rows):
        early, late = first_out[i], purified(1, i)
        for t in range(tiles):
            one, two = early[:, t * size:(t + 1) * size], late[:, t * size:(t + 1) * size]
            out_ref[i, 2 * t] = joined(one, swapped(two))
            out_ref[i, 2 * t + 1] = joined(swapped(one), two)
        pltpu.make_async_copy(out_ref.at[i], out_hbm.at[i], out_sem.at[i]).start()
    for spread in (w0, w1, q0, q1):
        spread.finish()
    for i in range(rows):
        pltpu.make_async_copy(out_ref.at[i], out_hbm.at[i], out_sem.at[i]).wait()


def solution(mesh):
    doms, row_devices = mesh.shape["dom"], mesh.shape["row"]
    assert row_devices == 4

    def per_device(p_blocks, p_cols, sel_square, sel_cube):
        rows, count, size, _ = p_blocks.shape
        products = sel_square.shape[1]
        tiles = products // 2
        flops = 2 * 2 * rows * products * count * size**3
        window_tiles = 2 * SLOTS * rows + 1
        square_tiles = 2 * SLOTS * rows * tiles + 1
        return pl.pallas_call(
            functools.partial(kernel, doms),
            out_shape=jax.ShapeDtypeStruct((rows, products, size, size), jnp.bfloat16),
            in_specs=[pl.BlockSpec(memory_space=pltpu.HBM)] * 4,
            out_specs=pl.BlockSpec(memory_space=pl.ANY),
            scratch_shapes=[
                pltpu.VMEM((rows, count, size, size), jnp.bfloat16),
                pltpu.SMEM(p_cols.shape, jnp.int32),
                pltpu.SMEM(sel_square.shape, jnp.int32),
                pltpu.SMEM(sel_cube.shape, jnp.int32),
                pltpu.SMEM((rows * count * products,), jnp.int32),
                pltpu.SMEM((rows * count * products,), jnp.int32),
                pltpu.VMEM((window_tiles, size, size), jnp.bfloat16),
                pltpu.VMEM((window_tiles, size, size), jnp.bfloat16),
                pltpu.VMEM((square_tiles, size, size), jnp.bfloat16),
                pltpu.VMEM((square_tiles, size, size), jnp.bfloat16),
                pltpu.VMEM((2, rows, size, tiles * size), jnp.float32),
                pltpu.VMEM((rows, size, tiles * size), jnp.bfloat16),
                pltpu.VMEM((rows, products, size, size), jnp.bfloat16),
                pltpu.SemaphoreType.DMA((5,)),
                pltpu.SemaphoreType.DMA((rows,)),
                pltpu.SemaphoreType.REGULAR,
                pltpu.SemaphoreType.DMA((2, 5, 2 * rows)),
                pltpu.SemaphoreType.DMA((2, 5, 2 * rows)),
                pltpu.SemaphoreType.DMA((2, 5, rows * tiles)),
                pltpu.SemaphoreType.DMA((2, 5, rows * tiles)),
            ],
            cost_estimate=pl.CostEstimate(flops=flops, bytes_accessed=4 * p_blocks.size, transcendentals=0),
            compiler_params=pltpu.CompilerParams(
                collective_id=0, has_side_effects=True, vmem_limit_bytes=60 * 1024 * 1024
            ),
        )(p_blocks, p_cols, sel_square, sel_cube)

    return jax.shard_map(
        per_device,
        mesh=mesh,
        in_specs=(
            P(("dom", "row"), None, None, None),
            P(("dom", "row"), None),
            P(("dom", "row"), None, None),
            P(("dom", "row"), None, None),
        ),
        out_specs=P(("dom", "row"), None, None, None),
        check_vma=False,
    )
```

```python
import functools

import jax
import jax.numpy as jnp
from jax import lax
from jax.experimental import pallas as pl
from jax.experimental.pallas import tpu as pltpu
from jax.sharding import PartitionSpec as P

MW = 2
REACH = 2
NEAR = 2 * REACH + 1
SLOTS = NEAR + 1
RIGHT, LEFT, OPPOSITE, ACROSS, SIDE = range(5)


class Spread:
    def __init__(self, buffer, chunks, sems, place):
        self.buffer, self.chunks = buffer, chunks
        self.send_sem, self.recv_sem = sems
        self.x, self.right, self.left, self.across, self.spot = place

    def copy(self, way, k):
        x = self.x
        cut, passed = self.chunks[k]
        opposite = 4 - 4 * (x // 2)
        if way == RIGHT:
            there = lax.rem(x + 1, 4)
            source, target, device = 2, 5 - 4 * ((there + 3) // 4), {"row": self.right}
        elif way == LEFT:
            there = lax.rem(x + 3, 4)
            source, target, device = 2, 3 + 2 * (there // 3), {"row": self.left}
        elif way == OPPOSITE:
            if passed == RIGHT:
                there = lax.rem(x + 1, 4)
                source, device = 5 - 4 * ((x + 3) // 4), {"row": self.right}
            else:
                there = lax.rem(x + 3, 4)
                source, device = 3 + 2 * (x // 3), {"row": self.left}
            target = 4 - 4 * (there // 2)
        elif way == ACROSS:
            source, target, device = opposite, 4 - opposite, {"dom": self.across}
        else:
            source, target, device = 5, 1 + 2 * (x // 3), {"dom": self.across}
        return pltpu.make_async_remote_copy(
            src_ref=cut(self.buffer, source),
            dst_ref=cut(self.buffer, target),
            send_sem=self.send_sem.at[way, k],
            recv_sem=self.recv_sem.at[way, k],
            device_id=device,
            device_id_type=pl.DeviceIdType.MESH,
        )

    def at_end(self, end, way, k, action):
        @pl.when(self.x == end)
        def _():
            getattr(self.copy(way, k), action)()

    def part(self, part):
        return range(len(self.chunks)) if part is None else part

    def send_passed(self, part=None):
        for k in self.part(part):
            self.copy(self.chunks[k][1], k).start()

    def send_urgent(self, part=None):
        for spot, way in ((0, LEFT), (7, RIGHT)):
            @pl.when(self.spot == spot)
            def _():
                for k in self.part(part):
                    if self.chunks[k][1] != way:
                        self.copy(way, k).start()

    def send_rest(self, part=None):
        for spot, way in ((0, LEFT), (7, RIGHT)):
            @pl.when(self.spot != spot)
            def _():
                for k in self.part(part):
                    if self.chunks[k][1] != way:
                        self.copy(way, k).start()

    def pass_on(self, part=None, sides=True):
        for k in self.part(part):
            self.copy(self.chunks[k][1], k).wait_recv()
            self.copy(OPPOSITE, k).start()
            if sides:
                self.send_sides((k,))

    def send_sides(self, part=None):
        for k in self.part(part):
            self.at_end(0 if self.chunks[k][1] == RIGHT else 3, SIDE, k, "start")

    def take_rest(self, part=None):
        for k in self.part(part):
            way = LEFT + RIGHT - self.chunks[k][1]
            self.copy(way, k).wait_recv()
            self.at_end(0 if way == RIGHT else 3, SIDE, k, "start")

    def send_across(self, part=None):
        for k in self.part(part):
            self.copy(OPPOSITE, k).wait_recv()
            self.copy(ACROSS, k).start()

    def take_across(self, part=None):
        for k in self.part(part):
            self.at_end(0, SIDE, k, "wait_recv")
            self.at_end(3, SIDE, k, "wait_recv")
            self.copy(ACROSS, k).wait_recv()

    def finish(self):
        for k in range(len(self.chunks)):
            for way in (RIGHT, LEFT, OPPOSITE, ACROSS):
                self.copy(way, k).wait_send()
            self.at_end(0, SIDE, k, "wait_send")
            self.at_end(3, SIDE, k, "wait_send")


def swapped(tile):
    half = tile.shape[1] // 2
    return jnp.concatenate([tile[:, half:], tile[:, :half]], axis=1)


def joined(first, second):
    half = first.shape[1] // 2
    return jnp.concatenate([first[:, :half], second[:, half:]], axis=1)


def place_picks(places, cols_ref, sel_ref, tiles, zero, origin, clusters, reach_rows):
    rows, products, count = sel_ref.shape
    turned = zero + 1

    def one(a, carry):
        for i in range(rows):
            near = cols_ref[i, a] - origin
            near = jnp.where(near < 0, near + clusters, near)
            near = jnp.where(near >= clusters, near - clusters, near)
            base = jnp.minimum(near, reach_rows - 1) * tiles
            for s in range(products):
                picked = sel_ref[i, s, a]
                odd = lax.bitwise_and(picked, 1)
                turn = odd if s % 2 == 0 else 1 - odd
                tile = base + lax.shift_right_arithmetic(picked, 1) + turned * turn
                places[(i * count + a) * products + s] = jnp.where(picked >= 0, tile, zero)
        return carry

    lax.fori_loop(0, count, one, 0)


def contract(blocks, nearby, places, row, products):
    count = blocks.shape[1]
    total = None
    for pair in range(0, count, 2):
        left = jnp.concatenate([blocks[row, pair], blocks[row, pair + 1]], axis=1)
        right = []
        for a in (pair, pair + 1):
            at = (row * count + a) * products
            line = [joined(nearby[places[at + s]], nearby[places[at + s + 1]]) for s in range(0, products, 2)]
            right.append(jnp.concatenate(line, axis=1))
        term = jnp.dot(left, jnp.concatenate(right, axis=0), preferred_element_type=jnp.float32)
        total = term if total is None else total + term
    return total


def kernel(
    doms, p_hbm, cols_hbm, sel_square_hbm, sel_cube_hbm, out_hbm,
    blocks, cols_ref, sel_square_ref, sel_cube_ref, window_places, square_places, window0, window1, square0, square1, total, first_out, out_ref,
    local_sem, out_sem, go_sem, window_send, window_recv, square_send, square_recv,
):
    rows, products, size = out_ref.shape[:3]
    half = size // 2
    x, dom = lax.axis_index("row"), lax.axis_index("dom")
    ahead, behind = lax.rem(dom + 1, doms), lax.rem(dom + doms - 1, doms)
    right, left = lax.rem(x + 1, 4), lax.rem(x + 3, 4)
    across = lax.rem(dom + doms + 1 - 2 * (x // 2), doms)
    clusters = doms * 4 * rows
    origin = ((dom * 4 + x) - REACH) * rows
    reach_rows = NEAR * rows

    own = pltpu.make_async_copy(p_hbm.at[:, pl.ds(0, MW)], blocks.at[:, pl.ds(0, MW)], local_sem.at[0])
    rest = blocks.shape[1] - MW
    others = [
        pltpu.make_async_copy(p_hbm.at[:, pl.ds(MW, rest)], blocks.at[:, pl.ds(MW, rest)], local_sem.at[1]),
        pltpu.make_async_copy(cols_hbm, cols_ref, local_sem.at[2]),
        pltpu.make_async_copy(sel_square_hbm, sel_square_ref, local_sem.at[3]),
        pltpu.make_async_copy(sel_cube_hbm, sel_cube_ref, local_sem.at[4]),
    ]
    own.start()
    for load in others:
        load.start()

    barrier = pltpu.get_barrier_semaphore()
    for device in ({"row": right}, {"row": left}, {"dom": behind}):
        pl.semaphore_signal(barrier, inc=1, device_id=device, device_id_type=pl.DeviceIdType.MESH)

    tiles = products // 2
    zero_w, zero_q = SLOTS * rows, SLOTS * rows * tiles
    windows, squares = (window0, window1), (square0, square1)
    for buffer, zero in ((window0, zero_w), (window1, zero_w), (square0, zero_q), (square1, zero_q)):
        buffer[zero] = jnp.zeros((size, size), buffer.dtype)
    own.wait()
    for i in range(rows):
        one, two = blocks[i, 0], blocks[i, 1]
        window0[REACH * rows + i] = joined(one, swapped(two))
        window1[REACH * rows + i] = joined(swapped(one), two)

    place = (x, right, left, across, x + 4 * lax.rem(dom, 2))

    def window_cut(tile, part):
        return lambda buffer, slot: buffer.at[slot * rows + tile, pl.ds(part * half, half)]

    def square_cut(tile):
        return lambda buffer, slot: buffer.at[slot * rows * tiles + tile]

    window_chunks = [(window_cut(tile, part), (RIGHT, LEFT)[part]) for tile in range(rows) for part in (0, 1)]
    square_chunks = [(square_cut(tile), RIGHT if tile % 2 == 0 else LEFT) for tile in range(rows * tiles)]
    w0, w1 = (Spread(windows[h], window_chunks, (window_send.at[h], window_recv.at[h]), place) for h in (0, 1))
    q0, q1 = (Spread(squares[h], square_chunks, (square_send.at[h], square_recv.at[h]), place) for h in (0, 1))

    def turn(buffer, unit, zero, slots):
        for slot in slots:
            for tile in range(unit):
                buffer[zero + 1 + slot * unit + tile] = swapped(buffer[slot * unit + tile])

    sooner = (2, 5 - 4 * ((x + 3) // 4), 3 + 2 * (x // 3), 4 - 4 * (x // 2))
    later = (4 * (x // 2), 1 + 2 * (x // 3))

    def make_square(h, spread):
        turn(windows[h], rows, zero_w, later)
        for i in range(rows):
            value = contract(blocks, windows[h], window_places, i, products)
            total[h, i] = value
            for t in range(tiles):
                squares[h][(REACH * rows + i) * tiles + t] = value[:, t * size:(t + 1) * size].astype(jnp.bfloat16)
            part = range(i * tiles, (i + 1) * tiles)
            spread.send_passed(part)
        spread.send_urgent()

    def purified(h, i):
        value = contract(blocks, squares[h], square_places, i, products)
        return (3.0 * total[h, i] - 2.0 * value).astype(out_ref.dtype)

    pl.semaphore_wait(barrier, 3)

    @pl.when(x >= 2)
    def _():
        pl.semaphore_signal(go_sem, inc=1, device_id={"dom": ahead}, device_id_type=pl.DeviceIdType.MESH)

    w0.send_passed()
    w0.send_urgent()
    w0.send_rest((0, 1))
    w0.pass_on((0, 1), False)
    w0.send_rest((2, 3))
    w0.pass_on((2, 3), False)
    w0.send_rest((4, 5))
    w0.pass_on((4, 5), False)
    w1.send_passed()
    w1.send_urgent()
    for load in others:
        load.wait()
    place_picks(window_places, cols_ref, sel_square_ref, 1, zero_w, origin, clusters, reach_rows)

    @pl.when(x >= 2)
    def _():
        pl.semaphore_wait(go_sem, 1)

    w0.send_sides()
    w0.take_rest()
    w0.send_across()
    w1.pass_on()
    w1.send_rest()
    place_picks(square_places, cols_ref, sel_cube_ref, tiles, zero_q, origin, clusters, reach_rows)
    turn(window0, rows, zero_w, sooner)
    w0.take_across()
    make_square(0, q0)
    w1.take_rest()
    w1.send_across()
    q0.pass_on()
    q0.send_rest()
    turn(window1, rows, zero_w, sooner)
    w1.take_across()
    make_square(1, q1)
    q0.send_across()
    q0.take_rest()
    q1.pass_on()
    q1.send_rest()
    q0.take_across()
    q1.send_across()
    q1.take_rest()
    turn(square0, rows * tiles, zero_q, sooner + later)
    for i in range(rows):
        first_out[i] = purified(0, i)
    turn(square1, rows * tiles, zero_q, sooner)
    q1.take_across()
    turn(square1, rows * tiles, zero_q, later)
    for i in range(rows):
        early, late = first_out[i], purified(1, i)
        for t in range(tiles):
            one, two = early[:, t * size:(t + 1) * size], late[:, t * size:(t + 1) * size]
            out_ref[i, 2 * t] = joined(one, swapped(two))
            out_ref[i, 2 * t + 1] = joined(swapped(one), two)
        pltpu.make_async_copy(out_ref.at[i], out_hbm.at[i], out_sem.at[i]).start()
    for spread in (w0, w1, q0, q1):
        spread.finish()
    for i in range(rows):
        pltpu.make_async_copy(out_ref.at[i], out_hbm.at[i], out_sem.at[i]).wait()


def solution(mesh):
    doms, row_devices = mesh.shape["dom"], mesh.shape["row"]
    assert row_devices == 4

    def per_device(p_blocks, p_cols, sel_square, sel_cube):
        rows, count, size, _ = p_blocks.shape
        products = sel_square.shape[1]
        tiles = products // 2
        flops = 2 * 2 * rows * products * count * size**3
        window_tiles = 2 * SLOTS * rows + 1
        square_tiles = 2 * SLOTS * rows * tiles + 1
        return pl.pallas_call(
            functools.partial(kernel, doms),
            out_shape=jax.ShapeDtypeStruct((rows, products, size, size), jnp.bfloat16),
            in_specs=[pl.BlockSpec(memory_space=pltpu.HBM)] * 4,
            out_specs=pl.BlockSpec(memory_space=pl.ANY),
            scratch_shapes=[
                pltpu.VMEM((rows, count, size, size), jnp.bfloat16),
                pltpu.SMEM(p_cols.shape, jnp.int32),
                pltpu.SMEM(sel_square.shape, jnp.int32),
                pltpu.SMEM(sel_cube.shape, jnp.int32),
                pltpu.SMEM((rows * count * products,), jnp.int32),
                pltpu.SMEM((rows * count * products,), jnp.int32),
                pltpu.VMEM((window_tiles, size, size), jnp.bfloat16),
                pltpu.VMEM((window_tiles, size, size), jnp.bfloat16),
                pltpu.VMEM((square_tiles, size, size), jnp.bfloat16),
                pltpu.VMEM((square_tiles, size, size), jnp.bfloat16),
                pltpu.VMEM((2, rows, size, tiles * size), jnp.float32),
                pltpu.VMEM((rows, size, tiles * size), jnp.bfloat16),
                pltpu.VMEM((rows, products, size, size), jnp.bfloat16),
                pltpu.SemaphoreType.DMA((5,)),
                pltpu.SemaphoreType.DMA((rows,)),
                pltpu.SemaphoreType.REGULAR,
                pltpu.SemaphoreType.DMA((2, 5, 2 * rows)),
                pltpu.SemaphoreType.DMA((2, 5, 2 * rows)),
                pltpu.SemaphoreType.DMA((2, 5, rows * tiles)),
                pltpu.SemaphoreType.DMA((2, 5, rows * tiles)),
            ],
            cost_estimate=pl.CostEstimate(flops=flops, bytes_accessed=4 * p_blocks.size, transcendentals=0),
            compiler_params=pltpu.CompilerParams(
                collective_id=0, has_side_effects=True, vmem_limit_bytes=60 * 1024 * 1024
            ),
        )(p_blocks, p_cols, sel_square, sel_cube)

    return jax.shard_map(
        per_device,
        mesh=mesh,
        in_specs=(
            P(("dom", "row"), None, None, None),
            P(("dom", "row"), None),
            P(("dom", "row"), None, None),
            P(("dom", "row"), None, None),
        ),
        out_specs=P(("dom", "row"), None, None, None),
        check_vma=False,
    )
```
